32 devices in a mesh: grp: 4 (over z), row: 8 (over y, x, core).
Axes of the slice: x: 2, y: 2, z: 4, core: 2. Of those that a mesh axis runs over, the one named last changes fastest.
Arguments:
- embeddings: bfloat16 [32768, 256], P(('grp', 'row')), may hold values from -6 to 6
- neighbour_tile_mask: int32 [128, 8, 256, 256], P(('grp', 'row')), may hold values 0 or 1
- column_blocks: int32 [128, 8], P(('grp', 'row')), may hold values from 0 to 31, as said below
- seed_labels: int32 [32768], P(('grp', 'row')), may hold values from 0 to 64, as said below
Outputs:
- label_scores: float32 [64, 32768], P(None, ('grp', 'row'))
The draws below stay inside these ranges and needn't reach their ends.
Inputs may be any that keep to these rules, and one draw needn't show every extreme that they name: `column_blocks`: entry [r, k] names a block of r's group (r // 32) by its index in that group; block b of a group lies on the group's device b // 4 along row. The 8 column blocks of one row-block lie on 8 different devices and never include r itself, so a device receives at most 4 mirrored tiles from one device, at most one from each of its row-blocks; in every draw each device has a device that receives exactly 4 from it. `seed_labels`: 64 marks a node without a seed label.
All inputs are finite; a program needn't handle non-finite values. No bound on the sum of `neighbour_tile_mask` on one device may be relied on, other than what follows from the above.
Results may differ from the reference program's by a relative error of at most 0.00041.
Values may be sent and summed in bfloat16 or wider, within the bound.
A program may use at most 128 MiB of HBM per device.

```python
import jax
import jax.numpy as jnp
from jax import lax

EMBEDDING_WIDTH = 256
CLASSES = 64
TILE_SIZE = 256
TILES_ROW = 8
STEPS = 2
BLOCKS_DEV = 4
GROUP_BLOCKS = 32
ROW_BLOCKS = 128
NODES = 32768
N_GRP = 4
N_ROW = 8


def draw_column_blocks(key, part):
    device_count = N_GRP * N_ROW
    key_favored, key_order, key_local, key_shift = jax.random.split(key, 4)
    favored = jax.random.randint(key_favored, (device_count, 1, 1), 0, N_ROW)
    peer_index = jnp.arange(N_ROW, dtype=jnp.int32)
    random_scores = jax.random.randint(key_order, (device_count, BLOCKS_DEV, N_ROW), 0, 1 << 20)
    ranking_scores = random_scores * N_ROW + peer_index
    ranking_scores = jnp.where(peer_index == favored, -1, ranking_scores)
    ranking = jnp.argsort(ranking_scores, axis=-1, stable=True).astype(jnp.int32)
    chosen = ranking[:, :, :TILES_ROW]
    local_block = jax.random.randint(key_local, (device_count, BLOCKS_DEV, TILES_ROW), 0, BLOCKS_DEV)
    shift_by = jax.random.randint(key_shift, (device_count, BLOCKS_DEV, TILES_ROW), 1, BLOCKS_DEV)
    self_member = (jnp.arange(device_count, dtype=jnp.int32) % N_ROW)[:, None, None]
    own_block = jnp.arange(BLOCKS_DEV, dtype=jnp.int32)[None, :, None]
    local_block = jnp.where(chosen == self_member, (own_block + shift_by) % BLOCKS_DEV, local_block)
    return (chosen * BLOCKS_DEV + local_block).reshape(ROW_BLOCKS, TILES_ROW).astype(jnp.int32)


def draw_seed_labels(key, part):
    key_chance, key_class = jax.random.split(key)
    position = jnp.arange(NODES, dtype=jnp.int32)
    chance = jax.random.randint(key_chance, (NODES,), 0, 1000)
    labeled = chance * NODES < 100 * NODES + 200 * position
    picked = jax.random.randint(key_class, (NODES,), 0, CLASSES)
    return jnp.where(labeled, picked, CLASSES).astype(jnp.int32)


def plant(array, stream_key, low, largest):
    longest = array.shape.index(max(array.shape))
    spots = []
    for shift in (0, 1):
        where = [jax.random.randint(jax.random.fold_in(stream_key, axis), (), 0, length) for axis, length in enumerate(array.shape)]
        where[longest] = (where[longest] + shift) % array.shape[longest]
        spots.append(tuple(where))
    return array.at[spots[0]].set(low).at[spots[1]].set(largest)


def level_of(rng, dims, cuts, low, top_value):
    level, own = 1.0, jax.random.fold_in(rng, 6)
    for dim, parts in cuts:
        steps = jnp.exp(jax.random.uniform(jax.random.fold_in(own, dim), (parts,), jnp.float32, low / len(cuts), top_value / len(cuts)))
        level = level * jnp.repeat(steps, dims[dim] // parts).reshape([-1 if axis == dim else 1 for axis in range(len(dims))])
    return level


def noise(key, shape, scale, bound, pieces=(), held_as=jnp.bfloat16):
    array = scale * jax.random.normal(key, shape, jnp.float32)
    if pieces:
        array = array * level_of(key, shape, pieces, -0.22, 0.18)
    return jnp.clip(array, -bound, bound).astype(held_as)


def setup_inputs(seed: int = 0) -> dict:
    keys = jax.random.split(jax.random.key(seed), 5)
    embeddings = noise(keys[0], (NODES, EMBEDDING_WIDTH), 1.0, 6.0, ((0, 32),))
    neighbour_tile_mask = plant((jax.random.randint(keys[1], (ROW_BLOCKS, TILES_ROW, TILE_SIZE, TILE_SIZE), 0, 4) < 3).astype(jnp.int32), jax.random.fold_in(keys[1], 1), 0, 1)
    column_blocks = draw_column_blocks(jax.random.fold_in(keys[4], 71), 0)
    seed_labels = draw_seed_labels(jax.random.fold_in(keys[4], 71), 0)
    return dict(embeddings=embeddings, neighbour_tile_mask=neighbour_tile_mask, column_blocks=column_blocks, seed_labels=seed_labels)


SOFTMAX_WARMTH = 0.1
PROPAGATION = 0.9

def reference(embeddings, neighbour_tile_mask, column_blocks, seed_labels):
    features = embeddings.astype(jnp.float32)
    unit_rows = (features * lax.rsqrt(lax.optimization_barrier(jnp.mean(features * features, axis=1, keepdims=True)) + 1e-06)).astype(jnp.bfloat16)
    unit_blocks = unit_rows.reshape(ROW_BLOCKS, TILE_SIZE, EMBEDDING_WIDTH)
    group_start = jnp.arange(ROW_BLOCKS, dtype=jnp.int32) // GROUP_BLOCKS * GROUP_BLOCKS
    global_cols = (group_start[:, None] + column_blocks).astype(jnp.int32)

    def tile_row(operand):
        own_block, columns, block_mask_tile = operand
        column_units = unit_blocks[columns]
        score_values = jnp.einsum('ie,kje->kij', own_block.astype(jnp.float32), column_units.astype(jnp.float32), precision=lax.Precision.HIGHEST)
        return jnp.where(block_mask_tile > 0, jnp.exp(score_values / (EMBEDDING_WIDTH * SOFTMAX_WARMTH)), jnp.zeros_like(score_values)).astype(jnp.bfloat16)
    affinity_matrix = lax.map(tile_row, (unit_blocks, global_cols, neighbour_tile_mask))
    row_sums = lax.optimization_barrier(jnp.sum(affinity_matrix, axis=(1, 3), dtype=jnp.float32))
    column_sums = lax.optimization_barrier(jnp.sum(affinity_matrix, axis=2, dtype=jnp.float32))
    mirror_degree = jax.ops.segment_sum(column_sums.reshape(ROW_BLOCKS * TILES_ROW, TILE_SIZE), global_cols.reshape(-1), num_segments=ROW_BLOCKS)
    degree = (1.0 + row_sums + mirror_degree).reshape(NODES)
    inverse_root = lax.rsqrt(degree)
    class_hits = (seed_labels[None, :] == jnp.arange(CLASSES, dtype=jnp.int32)[:, None]).astype(jnp.float32)
    counts = lax.optimization_barrier(jnp.sum(class_hits, axis=1))
    seed_field = class_hits * (NODES / (counts + 1.0))[:, None]
    label_field = seed_field
    for iteration in range(STEPS):
        spread = (label_field * inverse_root[None, :]).astype(jnp.bfloat16)
        spread_blocks = spread.reshape(CLASSES, ROW_BLOCKS, TILE_SIZE)

        def forward_row(operand):
            tiles_here, columns = operand
            column_spread = spread_blocks[:, columns]
            return jnp.einsum('kij,ckj->ci', tiles_here.astype(jnp.float32), column_spread.astype(jnp.float32), precision=lax.Precision.HIGHEST)

        def backward_row(operand):
            tiles_here, own_spread = operand
            product = jnp.einsum('kij,ci->kcj', tiles_here.astype(jnp.float32), own_spread.astype(jnp.float32), precision=lax.Precision.HIGHEST)
            return product.astype(jnp.bfloat16)
        forward = lax.map(forward_row, (affinity_matrix, global_cols))
        backward = lax.map(backward_row, (affinity_matrix, jnp.transpose(spread_blocks, (1, 0, 2)))).astype(jnp.float32)
        mirror = jax.ops.segment_sum(backward.reshape(ROW_BLOCKS * TILES_ROW, CLASSES, TILE_SIZE), global_cols.reshape(-1), num_segments=ROW_BLOCKS)
        summed = jnp.transpose(forward + mirror, (1, 0, 2)).reshape(CLASSES, NODES) + spread.astype(jnp.float32)
        label_field = PROPAGATION * inverse_root[None, :] * summed + (1.0 - PROPAGATION) * seed_field
    return label_field
```

```python
import functools
import math

import jax
import jax.numpy as jnp
from jax import lax
from jax.experimental import pallas as pl
from jax.experimental.pallas import tpu as pltpu
from jax.sharding import PartitionSpec as P

CLASSES = 64
STEPS = 2


SOFTMAX_WARMTH = 0.1
PROPAGATION = 0.9

BF = jnp.bfloat16
F32 = jnp.float32
NT = (((1,), (1,)), ((), ()))


def peer_of(me, offset):
    peer, bit = me, 1
    while bit <= offset:
        if offset & bit:
            peer = peer + bit * (1 - 2 * lax.rem(lax.div(me, bit), 2))
        bit *= 2
    return peer


def gather_plan(n):
    if n != 8:
        first = [(0, d, d, c) for d in range(1, n) for c in range(2)]
        events = []
        for d in range(1, n):
            events += [("wait", d, 0, []), ("wait", d, 1, []), ("use", d)]
        return first, events
    first = [(0, 2, 2, 0), (0, 4, 4, 1), (0, 2, 2, 1), (0, 4, 4, 0), (0, 1, 1, 0), (0, 1, 1, 1)]
    events = [
        ("wait", 1, 0, []),
        ("wait", 1, 1, []),
        ("use", 1),
        ("wait", 2, 0, [(2, 6, 4, 0), (2, 3, 1, 0)]),
        ("wait", 4, 1, [(4, 6, 2, 1), (4, 5, 1, 1)]),
        ("wait", 2, 1, [(2, 3, 1, 1)]),
        ("wait", 4, 0, [(4, 5, 1, 0)]),
        ("use", 2),
        ("use", 4),
        ("wait", 6, 0, [(6, 7, 1, 0)]),
        ("wait", 6, 1, [(6, 7, 1, 1)]),
        ("wait", 3, 0, []),
        ("wait", 3, 1, []),
        ("use", 3),
        ("wait", 5, 0, []),
        ("wait", 5, 1, []),
        ("use", 5),
        ("use", 6),
        ("wait", 7, 0, []),
        ("wait", 7, 1, []),
        ("use", 7),
    ]
    return first, events


def kernel(n, groups, node_total, cb, emb, mask_hbm, labels, out, *scratch):
    scratch = list(scratch)
    take = lambda count: [scratch.pop(0) for _ in range(count)]
    units = take(n)
    spreads = [take(n) for _ in range(STEPS)]
    (mask, aff, rows, terms_out, terms_in, msg_out, msg_in, cnt_out, cnt_in) = take(9)
    (grp_out, grp_in, pick, seed, total) = take(5)
    (mask_sem, unit_s, unit_r, spread_s, spread_r, term_s, term_r) = take(7)
    (msg_s, msg_r, cnt_s, cnt_r, grp_s, grp_r) = take(6)
    J, K, T, _ = mask.shape
    E = emb.shape[1]
    C = CLASSES
    me = lax.axis_index("row")
    my_group = lax.axis_index("grp")
    peers = [peer_of(me, d) for d in range(n)]
    sent = []

    def remote(src, dst, send, recv, device):
        return pltpu.make_async_remote_copy(
            src_ref=src, dst_ref=dst, send_sem=send, recv_sem=recv, device_id=device,
            device_id_type=pl.DeviceIdType.MESH,
        )

    def start(copy):
        copy.start()
        sent.append(copy)

    mask_copies = [
        pltpu.make_async_copy(mask_hbm.at[j], mask.at[j], mask_sem.at[j]) for j in range(J)
    ]
    for copy in mask_copies:
        copy.start()
    barrier = pltpu.get_barrier_semaphore()
    for d in range(1, n):
        pl.semaphore_signal(
            barrier, inc=1, device_id={"row": peers[d]}, device_id_type=pl.DeviceIdType.MESH
        )
    others = [lax.rem(my_group + g, groups) for g in range(groups)]
    for g in range(1, groups):
        pl.semaphore_signal(
            barrier, inc=1, device_id={"grp": others[g]}, device_id_type=pl.DeviceIdType.MESH
        )

    def normalise(j, carry):
        features = emb[pl.ds(pl.multiple_of(j * T, T), T), :].astype(F32)
        mean = jnp.mean(features * features, axis=1, keepdims=True)
        units[0][j] = (features * lax.rsqrt(mean + 1e-06)).astype(BF)
        return carry

    lax.fori_loop(0, J, normalise, 0)
    pl.semaphore_wait(barrier, n - 1 + groups - 1)

    half = J // 2
    first, events = gather_plan(n)

    def gather_copy(slots, send, recv, move):
        src, dst, via, part = move
        piece = pl.ds(part * half, half)
        return remote(
            slots[src].at[piece], slots[dst].at[piece], send.at[dst, part], recv.at[dst, part],
            {"row": peers[via]},
        )

    def gather_start(slots, send, recv):
        for move in first:
            start(gather_copy(slots, send, recv, move))

    def gather_finish(slots, send, recv, use):
        for event in events:
            if event[0] == "use":
                use(event[1])
                continue
            _, slot, part, moves = event
            gather_copy(slots, send, recv, (0, slot, slot, part)).wait_recv()
            for move in moves:
                start(gather_copy(slots, send, recv, move))

    gather_start(units, unit_s, unit_r)

    wide = -(-C // 128) * 128
    ones_rows = jnp.ones((8, T), BF)
    count = jnp.zeros((8, wide), F32)
    for j in range(J):
        classes = lax.broadcasted_iota(jnp.int32, (wide, T), 0)
        hits = jnp.where(labels[:, j * T:(j + 1) * T] == classes, 1.0, 0.0).astype(BF)
        count += lax.dot_general(ones_rows, hits, NT, preferred_element_type=F32)
    cnt_out[...] = count
    cnt_copies = [None] + [
        remote(cnt_out, cnt_in.at[d], cnt_s.at[d], cnt_r.at[d], {"row": peers[d]})
        for d in range(1, n)
    ]
    for copy in cnt_copies[1:]:
        start(copy)

    def locate(j, d):
        slot, block, here = jnp.int32(0), jnp.int32(0), jnp.int32(0)
        base = peers[d] * J
        for k in range(K):
            at = cb[j, k] - base
            hit = jnp.logical_and(at >= 0, at < J)
            slot = jnp.where(hit, k, slot)
            block = jnp.where(hit, at, block)
            here = jnp.where(hit, 1, here)
        return slot, block, here

    lanes = lax.broadcasted_iota(jnp.int32, (8, J * C), 1)
    sublanes = lax.broadcasted_iota(jnp.int32, (8, T), 0)
    factor = math.log2(math.e) / (E * SOFTMAX_WARMTH)

    def tiles(d):
        def body(j, carry):
            column_sums, target_rows = carry
            slot, block, here = locate(j, d)
            score = lax.dot_general(
                units[0][j], units[d][block], NT, preferred_element_type=F32
            )
            tile = jnp.where(mask[j, slot] > 1 - here, jnp.exp2(score * factor), 0.0).astype(BF)
            aff[d, j] = tile
            row = lax.dot_general(ones_rows, tile, NT, preferred_element_type=F32)
            rows[j] = row if d == 0 else rows[j] + row
            column = jnp.dot(ones_rows, tile, preferred_element_type=F32)
            column_sums += jnp.where(sublanes == block, column, 0.0)
            inside = jnp.logical_and(lanes >= j * C, lanes < (j + 1) * C)
            target_rows = jnp.where(inside, lanes + (block - j) * C, target_rows)
            return column_sums, target_rows

        column_sums, target_rows = lax.fori_loop(
            0, J, body, (jnp.zeros((8, T), F32), jnp.zeros((8, J * C), jnp.int32))
        )
        own = msg_in if d == 0 else msg_out
        own[d, 0:8, 0:T] = column_sums
        own[d, 8:16, 0:J * C] = target_rows.astype(F32)
        if d:
            start(msg_copy(d))

    def msg_copy(d):
        return remote(msg_out.at[d], msg_in.at[d], msg_s.at[d], msg_r.at[d], {"row": peers[d]})

    for copy in mask_copies:
        copy.wait()
    tiles(0)

    for d in range(1, n):
        cnt_copies[d].wait_recv()
        count += cnt_in[d]
    grp_out[...] = count
    grp_copies = [
        remote(grp_out, grp_in.at[g], grp_s.at[g], grp_r.at[g], {"grp": others[g]})
        for g in range(1, groups)
    ]
    for copy in grp_copies:
        start(copy)

    gather_finish(units, unit_s, unit_r, tiles)

    for g in range(1, groups):
        grp_copies[g - 1].wait_recv()
        count += grp_in[g]
    weight = jnp.transpose(jnp.broadcast_to((node_total / (count + 1.0))[0:1, :], (wide, wide)))
    weight = weight[0:C, 0:1]
    for j in range(J):
        classes = lax.broadcasted_iota(jnp.int32, (C, T), 0)
        hits = jnp.where(labels[:, j * T:(j + 1) * T] == classes, 1.0, 0.0)
        seed[j] = hits * weight

    mirror_degree = msg_in[0, 0:8, 0:T]
    row_index = lax.broadcasted_iota(jnp.int32, (J * C, J * C), 0).astype(F32)
    for d in range(n):
        if d:
            msg_copy(d).wait_recv()
            mirror_degree += msg_in[d, 0:8, 0:T]
        pick[d] = jnp.where(row_index == msg_in[d, 8:9, 0:J * C], 1.0, 0.0).astype(BF)
    inverse_root = [
        lax.rsqrt(1.0 + rows[j][0:1, :] + mirror_degree[j:j + 1, :]) for j in range(J)
    ]

    order = sorted(range(1, n), reverse=True)
    for step in range(STEPS):
        slots = spreads[step]
        for j in range(J):
            field = seed[j] if step == 0 else total[j]
            slots[0][j] = (field * inverse_root[j]).astype(BF)
        gather_start(slots, spread_s.at[step], spread_r.at[step])

        def term_copy(d):
            return remote(
                terms_out.at[step, d], terms_in.at[step, d], term_s.at[step, d],
                term_r.at[step, d], {"row": peers[d]},
            )

        def mirror(d):
            for j in range(J):
                terms_out[step, d, j] = jnp.dot(
                    slots[0][j], aff[d, j], preferred_element_type=F32
                ).astype(BF)

        def forward(d):
            def body(j, carry):
                _, block, _ = locate(j, d)
                term = lax.dot_general(
                    slots[d][block], aff[d, j], NT, preferred_element_type=F32
                )
                total[j] = term if d == 0 else total[j] + term
                return carry

            lax.fori_loop(0, J, body, 0)

        for d in order:
            mirror(d)
            start(term_copy(d))
        mirror(0)
        forward(0)
        gather_finish(slots, spread_s.at[step], spread_r.at[step], forward)
        mirrored = jnp.dot(
            pick[0], terms_out[step, 0].reshape(J * C, T), preferred_element_type=F32
        )
        for d in range(1, n):
            term_copy(d).wait_recv()
            mirrored += jnp.dot(
                pick[d], terms_in[step, d].reshape(J * C, T), preferred_element_type=F32
            )
        for j in range(J):
            summed = total[j] + mirrored[j * C:(j + 1) * C, :] + slots[0][j].astype(F32)
            field = PROPAGATION * inverse_root[j] * summed + (1.0 - PROPAGATION) * seed[j]
            if step == STEPS - 1:
                out[:, j * T:(j + 1) * T] = field
            else:
                total[j] = field

    for copy in sent:
        copy.wait_send()


def local(embeddings, neighbour_tile_mask, column_blocks, seed_labels):
    J, K, T, _ = neighbour_tile_mask.shape
    E = embeddings.shape[1]
    C = CLASSES
    n = lax.axis_size("row")
    groups = lax.axis_size("grp")
    node_total = embeddings.shape[0] * n * groups
    wide = -(-C // 128) * 128
    width = max(T, J * C)
    dma = pltpu.SemaphoreType.DMA
    scratch = [pltpu.VMEM((J, T, E), BF) for _ in range(n)]
    scratch += [pltpu.VMEM((J, C, T), BF) for _ in range(n * STEPS)]
    scratch += [
        pltpu.VMEM((J, K, T, T), jnp.int32),
        pltpu.VMEM((n, J, T, T), BF),
        pltpu.VMEM((J, 8, T), F32),
        pltpu.VMEM((STEPS, n, J, C, T), BF),
        pltpu.VMEM((STEPS, n, J, C, T), BF),
        pltpu.VMEM((n, 16, width), F32),
        pltpu.VMEM((n, 16, width), F32),
        pltpu.VMEM((8, wide), F32),
        pltpu.VMEM((n, 8, wide), F32),
        pltpu.VMEM((8, wide), F32),
        pltpu.VMEM((groups, 8, wide), F32),
        pltpu.VMEM((n, J * C, J * C), BF),
        pltpu.VMEM((J, C, T), F32),
        pltpu.VMEM((J, C, T), F32),
        dma((J,)),
        dma((n, 2)), dma((n, 2)),
        dma((STEPS, n, 2)), dma((STEPS, n, 2)),
        dma((STEPS, n)), dma((STEPS, n)),
        dma((n,)), dma((n,)),
        dma((n,)), dma((n,)),
        dma((groups,)), dma((groups,)),
    ]
    vmem = pl.BlockSpec(memory_space=pltpu.VMEM)
    return pl.pallas_call(
        functools.partial(kernel, n, groups, node_total),
        out_shape=jax.ShapeDtypeStruct((C, J * T), F32),
        in_specs=[
            pl.BlockSpec(memory_space=pltpu.SMEM),
            vmem,
            pl.BlockSpec(memory_space=pl.ANY),
            vmem,
        ],
        out_specs=vmem,
        scratch_shapes=scratch,
        compiler_params=pltpu.CompilerParams(
            collective_id=0, has_side_effects=True, vmem_limit_bytes=56 * 1024 * 1024
        ),
    )(column_blocks, embeddings, neighbour_tile_mask, seed_labels.reshape(1, -1))


def solution(mesh):
    return jax.shard_map(
        local,
        mesh=mesh,
        in_specs=(
            P(("grp", "row"), None),
            P(("grp", "row"), None, None, None),
            P(("grp", "row"), None),
            P(("grp", "row")),
        ),
        out_specs=P(None, ("grp", "row")),
        check_vma=False,
    )
```

```python
import functools
import math

import jax
import jax.numpy as jnp
from jax import lax
from jax.experimental import pallas as pl
from jax.experimental.pallas import tpu as pltpu
from jax.sharding import PartitionSpec as P

CLASSES = 64
STEPS = 2


SOFTMAX_WARMTH = 0.1
PROPAGATION = 0.9

BF = jnp.bfloat16
F32 = jnp.float32
NT = (((1,), (1,)), ((), ()))


def peer_of(me, offset):
    peer, bit = me, 1
    while bit <= offset:
        if offset & bit:
            peer = peer + bit * (1 - 2 * lax.rem(lax.div(me, bit), 2))
        bit *= 2
    return peer


def gather_plan(n):
    if n != 8:
        first = [(0, d, d, c) for d in range(1, n) for c in range(2)]
        events = []
        for d in range(1, n):
            events += [("wait", d, 0, []), ("wait", d, 1, []), ("use", d)]
        return first, events
    first = [(0, 2, 2, 0), (0, 4, 4, 1), (0, 2, 2, 1), (0, 4, 4, 0), (0, 1, 1, 0), (0, 1, 1, 1)]
    events = [
        ("wait", 1, 0, []),
        ("wait", 1, 1, []),
        ("wait", 2, 0, [(2, 6, 4, 0), (2, 3, 1, 0)]),
        ("wait", 4, 1, [(4, 6, 2, 1), (4, 5, 1, 1)]),
        ("wait", 2, 1, [(2, 3, 1, 1)]),
        ("wait", 4, 0, [(4, 5, 1, 0)]),
        ("use", 1),
        ("use", 2),
        ("use", 4),
        ("wait", 6, 0, [(6, 7, 1, 0)]),
        ("wait", 6, 1, [(6, 7, 1, 1)]),
        ("wait", 3, 0, []),
        ("wait", 3, 1, []),
        ("use", 3),
        ("wait", 5, 0, []),
        ("wait", 5, 1, []),
        ("use", 5),
        ("use", 6),
        ("wait", 7, 0, []),
        ("wait", 7, 1, []),
        ("use", 7),
    ]
    return first, events


def kernel(n, groups, node_total, cb, emb, mask_hbm, labels, out, *scratch):
    scratch = list(scratch)
    take = lambda count: [scratch.pop(0) for _ in range(count)]
    units = take(n)
    spreads = [take(n) for _ in range(STEPS)]
    (mask, aff, rows, terms_out, terms_in, msg_out, msg_in, cnt_out, cnt_in) = take(9)
    (grp_out, grp_in, pick, seed, total) = take(5)
    (mask_sem, unit_s, unit_r, spread_s, spread_r, term_s, term_r) = take(7)
    (msg_s, msg_r, cnt_s, cnt_r, grp_s, grp_r) = take(6)
    J, K, T, _ = mask.shape
    E = emb.shape[1]
    C = CLASSES
    me = lax.axis_index("row")
    my_group = lax.axis_index("grp")
    peers = [peer_of(me, d) for d in range(n)]
    sent = []

    def remote(src, dst, send, recv, device):
        return pltpu.make_async_remote_copy(
            src_ref=src, dst_ref=dst, send_sem=send, recv_sem=recv, device_id=device,
            device_id_type=pl.DeviceIdType.MESH,
        )

    def start(copy):
        copy.start()
        sent.append(copy)

    mask_copies = [
        pltpu.make_async_copy(mask_hbm.at[j], mask.at[j], mask_sem.at[j]) for j in range(J)
    ]
    for copy in mask_copies:
        copy.start()
    barrier = pltpu.get_barrier_semaphore()
    for d in range(1, n):
        pl.semaphore_signal(
            barrier, inc=1, device_id={"row": peers[d]}, device_id_type=pl.DeviceIdType.MESH
        )
    others = [lax.rem(my_group + g, groups) for g in range(groups)]
    for g in range(1, groups):
        pl.semaphore_signal(
            barrier, inc=1, device_id={"grp": others[g]}, device_id_type=pl.DeviceIdType.MESH
        )

    def normalise(j, carry):
        features = emb[pl.ds(pl.multiple_of(j * T, T), T), :].astype(F32)
        mean = jnp.mean(features * features, axis=1, keepdims=True)
        units[0][j] = (features * lax.rsqrt(mean + 1e-06)).astype(BF)
        return carry

    lax.fori_loop(0, J, normalise, 0)
    pl.semaphore_wait(barrier, n - 1 + groups - 1)

    half = J // 2
    first, events = gather_plan(n)

    def gather_copy(slots, send, recv, move):
        src, dst, via, part = move
        piece = pl.ds(part * half, half)
        return remote(
            slots[src].at[piece], slots[dst].at[piece], send.at[dst, part], recv.at[dst, part],
            {"row": peers[via]},
        )

    def gather_start(slots, send, recv):
        for move in first:
            start(gather_copy(slots, send, recv, move))

    def gather_finish(slots, send, recv, use):
        for event in events:
            if event[0] == "use":
                use(event[1])
                continue
            _, slot, part, moves = event
            gather_copy(slots, send, recv, (0, slot, slot, part)).wait_recv()
            for move in moves:
                start(gather_copy(slots, send, recv, move))

    gather_start(units, unit_s, unit_r)

    wide = -(-C // 128) * 128
    ones_rows = jnp.ones((8, T), BF)
    count = jnp.zeros((8, wide), F32)
    for j in range(J):
        classes = lax.broadcasted_iota(jnp.int32, (wide, T), 0)
        hits = jnp.where(labels[:, j * T:(j + 1) * T] == classes, 1.0, 0.0).astype(BF)
        count += lax.dot_general(ones_rows, hits, NT, preferred_element_type=F32)
    cnt_out[...] = count
    cnt_copies = [None] + [
        remote(cnt_out, cnt_in.at[d], cnt_s.at[d], cnt_r.at[d], {"row": peers[d]})
        for d in range(1, n)
    ]
    for copy in cnt_copies[1:]:
        start(copy)

    def locate(j, d):
        slot, block, here = jnp.int32(0), jnp.int32(0), jnp.int32(0)
        base = peers[d] * J
        for k in range(K):
            at = cb[j, k] - base
            hit = jnp.logical_and(at >= 0, at < J)
            slot = jnp.where(hit, k, slot)
            block = jnp.where(hit, at, block)
            here = jnp.where(hit, 1, here)
        return slot, block, here

    lanes = lax.broadcasted_iota(jnp.int32, (8, J * C), 1)
    sublanes = lax.broadcasted_iota(jnp.int32, (8, T), 0)
    factor = math.log2(math.e) / (E * SOFTMAX_WARMTH)

    def tiles(d):
        def body(j, carry):
            column_sums, target_rows = carry
            slot, block, here = locate(j, d)
            score = lax.dot_general(
                units[0][j], units[d][block], NT, preferred_element_type=F32
            )
            tile = jnp.where(mask[j, slot] > 1 - here, jnp.exp2(score * factor), 0.0).astype(BF)
            aff[d, j] = tile
            row = lax.dot_general(ones_rows, tile, NT, preferred_element_type=F32)
            rows[j] = row if d == 0 else rows[j] + row
            column = jnp.dot(ones_rows, tile, preferred_element_type=F32)
            column_sums += jnp.where(sublanes == block, column, 0.0)
            inside = jnp.logical_and(lanes >= j * C, lanes < (j + 1) * C)
            target_rows = jnp.where(inside, lanes + (block - j) * C, target_rows)
            return column_sums, target_rows

        column_sums, target_rows = lax.fori_loop(
            0, J, body, (jnp.zeros((8, T), F32), jnp.zeros((8, J * C), jnp.int32)),
            unroll=True,
        )
        own = msg_in if d == 0 else msg_out
        own[d, 0:8, 0:T] = column_sums
        own[d, 8:16, 0:J * C] = target_rows.astype(F32)
        if d:
            start(msg_copy(d))

    def msg_copy(d):
        return remote(msg_out.at[d], msg_in.at[d], msg_s.at[d], msg_r.at[d], {"row": peers[d]})

    for copy in mask_copies:
        copy.wait()
    tiles(0)

    for d in range(1, n):
        cnt_copies[d].wait_recv()
        count += cnt_in[d]
    grp_out[...] = count
    grp_copies = [
        remote(grp_out, grp_in.at[g], grp_s.at[g], grp_r.at[g], {"grp": others[g]})
        for g in range(1, groups)
    ]
    for copy in grp_copies:
        start(copy)

    gather_finish(units, unit_s, unit_r, tiles)

    for g in range(1, groups):
        grp_copies[g - 1].wait_recv()
        count += grp_in[g]
    weight = jnp.transpose(jnp.broadcast_to((node_total / (count + 1.0))[0:1, :], (wide, wide)))
    weight = weight[0:C, 0:1]
    for j in range(J):
        classes = lax.broadcasted_iota(jnp.int32, (C, T), 0)
        hits = jnp.where(labels[:, j * T:(j + 1) * T] == classes, 1.0, 0.0)
        seed[j] = hits * weight

    mirror_degree = msg_in[0, 0:8, 0:T]
    row_index = lax.broadcasted_iota(jnp.int32, (J * C, J * C), 0).astype(F32)
    for d in range(n):
        if d:
            msg_copy(d).wait_recv()
            mirror_degree += msg_in[d, 0:8, 0:T]
        pick[d] = jnp.where(row_index == msg_in[d, 8:9, 0:J * C], 1.0, 0.0).astype(BF)
    inverse_root = [
        lax.rsqrt(1.0 + rows[j][0:1, :] + mirror_degree[j:j + 1, :]) for j in range(J)
    ]

    order = sorted(range(1, n), reverse=True)
    for step in range(STEPS):
        slots = spreads[step]
        for j in range(J):
            field = seed[j] if step == 0 else total[j]
            slots[0][j] = (field * inverse_root[j]).astype(BF)
        gather_start(slots, spread_s.at[step], spread_r.at[step])

        def term_copy(d):
            return remote(
                terms_out.at[step, d], terms_in.at[step, d], term_s.at[step, d],
                term_r.at[step, d], {"row": peers[d]},
            )

        def mirror(d):
            for j in range(J):
                terms_out[step, d, j] = jnp.dot(
                    slots[0][j], aff[d, j], preferred_element_type=F32
                ).astype(BF)

        def forward(d):
            def body(j, carry):
                _, block, _ = locate(j, d)
                term = lax.dot_general(
                    slots[d][block], aff[d, j], NT, preferred_element_type=F32
                )
                total[j] = term if d == 0 else total[j] + term
                return carry

            lax.fori_loop(0, J, body, 0, unroll=True)

        for d in order:
            mirror(d)
            start(term_copy(d))

        def use(d):
            if d == 1:
                mirror(0)
                forward(0)
            forward(d)

        gather_finish(slots, spread_s.at[step], spread_r.at[step], use)
        mirrored = jnp.dot(
            pick[0], terms_out[step, 0].reshape(J * C, T), preferred_element_type=F32
        )
        for d in range(1, n):
            term_copy(d).wait_recv()
            mirrored += jnp.dot(
                pick[d], terms_in[step, d].reshape(J * C, T), preferred_element_type=F32
            )
        for j in range(J):
            summed = total[j] + mirrored[j * C:(j + 1) * C, :] + slots[0][j].astype(F32)
            field = PROPAGATION * inverse_root[j] * summed + (1.0 - PROPAGATION) * seed[j]
            if step == STEPS - 1:
                out[:, j * T:(j + 1) * T] = field
            else:
                total[j] = field

    for copy in sent:
        copy.wait_send()


def local(embeddings, neighbour_tile_mask, column_blocks, seed_labels):
    J, K, T, _ = neighbour_tile_mask.shape
    E = embeddings.shape[1]
    C = CLASSES
    n = lax.axis_size("row")
    groups = lax.axis_size("grp")
    node_total = embeddings.shape[0] * n * groups
    wide = -(-C // 128) * 128
    width = max(T, J * C)
    dma = pltpu.SemaphoreType.DMA
    scratch = [pltpu.VMEM((J, T, E), BF) for _ in range(n)]
    scratch += [pltpu.VMEM((J, C, T), BF) for _ in range(n * STEPS)]
    scratch += [
        pltpu.VMEM((J, K, T, T), jnp.int32),
        pltpu.VMEM((n, J, T, T), BF),
        pltpu.VMEM((J, 8, T), F32),
        pltpu.VMEM((STEPS, n, J, C, T), BF),
        pltpu.VMEM((STEPS, n, J, C, T), BF),
        pltpu.VMEM((n, 16, width), F32),
        pltpu.VMEM((n, 16, width), F32),
        pltpu.VMEM((8, wide), F32),
        pltpu.VMEM((n, 8, wide), F32),
        pltpu.VMEM((8, wide), F32),
        pltpu.VMEM((groups, 8, wide), F32),
        pltpu.VMEM((n, J * C, J * C), BF),
        pltpu.VMEM((J, C, T), F32),
        pltpu.VMEM((J, C, T), F32),
        dma((J,)),
        dma((n, 2)), dma((n, 2)),
        dma((STEPS, n, 2)), dma((STEPS, n, 2)),
        dma((STEPS, n)), dma((STEPS, n)),
        dma((n,)), dma((n,)),
        dma((n,)), dma((n,)),
        dma((groups,)), dma((groups,)),
    ]
    vmem = pl.BlockSpec(memory_space=pltpu.VMEM)
    return pl.pallas_call(
        functools.partial(kernel, n, groups, node_total),
        out_shape=jax.ShapeDtypeStruct((C, J * T), F32),
        in_specs=[
            pl.BlockSpec(memory_space=pltpu.SMEM),
            vmem,
            pl.BlockSpec(memory_space=pl.ANY),
            vmem,
        ],
        out_specs=vmem,
        scratch_shapes=scratch,
        compiler_params=pltpu.CompilerParams(
            collective_id=0, has_side_effects=True, vmem_limit_bytes=56 * 1024 * 1024
        ),
    )(column_blocks, embeddings, neighbour_tile_mask, seed_labels.reshape(1, -1))


def solution(mesh):
    return jax.shard_map(
        local,
        mesh=mesh,
        in_specs=(
            P(("grp", "row"), None),
            P(("grp", "row"), None, None, None),
            P(("grp", "row"), None),
            P(("grp", "row")),
        ),
        out_specs=P(None, ("grp", "row")),
        check_vma=False,
    )
```
